512 devices in a mesh: row: 16 (over y, x), col: 32 (over z, core).
Axes of the slice: x: 4, y: 4, z: 16, core: 2. Of those that a mesh axis runs over, the one named last changes fastest.
Arguments:
- factor_panel: bfloat16 [2, 2048, 98304], P(None, 'row', 'col'), may hold values from -0.01953125 to 0.01953125
- solved_earlier: bfloat16 [1024, 98304], P('row', 'col'), may hold values from -6 to 6
- right_side: bfloat16 [2, 2048, 1024], P(None, 'row'), may hold values from -6 to 6
- coupling: bfloat16 [2048, 2048], P('row', 'col'), may hold values from -0.125 to 0.125
- inverses: bfloat16 [2, 2048, 2048], P(None, 'col', 'row'), as said below
Outputs:
- solved: bfloat16 [2, 2048, 1024], P(None, 'col')
The draws below stay inside these ranges and needn't reach their ends.
Inputs may be any that keep to these rules, and one draw needn't show every extreme that they name: `inverses`: each of the two blocks is lower triangular with a positive diagonal.
All inputs are finite; a program needn't handle non-finite values.
Results may differ from the reference program's by a relative error of at most 0.006.
Values may be sent and summed in bfloat16 or wider, within the bound.
No kernel may reach another device: no remote copies, remote signals or barrier semaphores. Data moves between devices by JAX's collectives and lax.ppermute only.
A program may use at most 64 MiB of HBM per device.

```python
import math
import jax
import jax.numpy as jnp

BS = 2048
NRHS = 1024
PREV = 98304


def draw_inverses(key, part):
    key = jax.random.fold_in(key, 7)
    key_diag, key_off = jax.random.split(key)
    diag_vals = jnp.exp(jax.random.uniform(key_diag, (2, BS), jnp.float32, math.log(0.5), math.log(2.0)))
    off_vals = jax.random.normal(key_off, (2, BS, BS), jnp.float32)
    off_vals = off_vals * float(BS) ** (-0.5)
    row_ids = jnp.arange(BS, dtype=jnp.int32)[:, None]
    col_ids = jnp.arange(BS, dtype=jnp.int32)[None, :]
    lower = (row_ids > col_ids)[None, :, :]
    on_diag = (row_ids == col_ids)[None, :, :]
    result = jnp.where(lower, off_vals, 0.0) + jnp.where(on_diag, diag_vals[:, :, None], 0.0)
    return result.astype(jnp.bfloat16)


def block_scale(rng, dims, pieces, least, high):
    loudness = 1.0
    for dim, parts in pieces:
        draws = jax.random.uniform(jax.random.fold_in(jax.random.fold_in(rng, 6), dim), (parts,), jnp.float32, least / len(pieces), high / len(pieces))
        loudness = loudness * jnp.repeat(jnp.exp(draws), dims[dim] // parts).reshape((-1,) + (1,) * (len(dims) - 1 - dim))
    return loudness


def noise(stream_key, extent, spread, most, cuts=(), held_as=jnp.bfloat16):
    loudness = block_scale(stream_key, extent, cuts, -0.22, 0.18) if cuts else 1.0
    entries = jax.random.normal(stream_key, extent, jnp.float32) * spread * loudness
    return jnp.minimum(jnp.maximum(entries, -most), most).astype(held_as)


def setup_inputs(seed: int = 0) -> dict:
    streams_of = jax.random.split(jax.random.key(seed), 6)
    factor_panel = noise(streams_of[0], (2, BS, PREV), PREV ** -0.5, 0.01953125, ((1, 16), (2, 32)))
    solved_earlier = noise(streams_of[1], (NRHS, PREV), 1.0, 6.0, ((0, 16), (1, 32)))
    right_side = noise(streams_of[2], (2, BS, NRHS), 1.0, 6.0, ((1, 16),))
    coupling = noise(streams_of[3], (BS, BS), BS ** -0.5, 0.125, ((0, 16), (1, 32)))
    inverses = draw_inverses(jax.random.fold_in(streams_of[5], 71), 0)
    return {"factor_panel": factor_panel, "solved_earlier": solved_earlier, "right_side": right_side, "coupling": coupling, "inverses": inverses}


def reference(factor_panel, solved_earlier, right_side, coupling, inverses):
    earlier = solved_earlier.T
    prefix_first = jnp.dot(factor_panel[0], earlier, preferred_element_type=jnp.float32)
    prefix_second = jnp.dot(factor_panel[1], earlier, preferred_element_type=jnp.float32)
    residual_first = (right_side[0].astype(jnp.float32) - prefix_first).astype(jnp.bfloat16)
    solved_first = jnp.dot(inverses[0], residual_first, preferred_element_type=jnp.float32).astype(jnp.bfloat16)
    cross_term = jnp.dot(coupling, solved_first, preferred_element_type=jnp.float32)
    residual_second = (right_side[1].astype(jnp.float32) - (prefix_second + cross_term)).astype(jnp.bfloat16)
    solved_second = jnp.dot(inverses[1], residual_second, preferred_element_type=jnp.float32).astype(jnp.bfloat16)
    return jnp.stack([solved_first, solved_second])
```

```python
import jax
import jax.numpy as jnp
from jax import lax
from jax.sharding import Mesh, PartitionSpec as P

BF16 = jnp.bfloat16
F32 = jnp.float32


def spread(block, axis, size):
    copies = jnp.broadcast_to(block[None], (size,) + block.shape)
    return lax.all_to_all(copies, axis, 0, 0)


def sum_rows(terms, axis, size):
    rows, cols = terms.shape
    pieces = lax.all_to_all(terms.reshape(size, rows // size, cols), axis, 0, 0)
    return jnp.sum(pieces.astype(F32), axis=0)


def swap_cores(block):
    return lax.ppermute(block, "core", [(0, 1), (1, 0)])


def matmul(a, b, contract):
    return lax.dot_general(a, b, ((contract[0:1], contract[1:2]), ((), ())), preferred_element_type=F32)


def make_per_device(n_row, n_z):
    def per_device(factor_panel, solved_earlier, right_side, coupling, inverses):
        core = lax.axis_index("core")
        z = lax.axis_index("z")
        blocks, rows, depth = factor_panel.shape
        own = coupling.shape[1]

        earlier = lax.all_gather(solved_earlier, "row", axis=0, tiled=True)

        packed = jnp.concatenate([coupling.T, inverses[0]], axis=0)
        mine = spread(packed, "z", n_z)
        other = swap_cores(mine)

        def pick(part, first):
            return part[:, :own] if first else part[:, own:]

        left = [
            matmul(inverses[1], pick(part, True).reshape(-1, rows), (1, 1)).astype(BF16)
            for part in (mine, other)
        ]
        left = spread(sum_rows(jnp.concatenate(left, axis=0), "row", n_row).astype(BF16), "row", n_row)
        left = left.reshape(2, own, -1)
        cross = -(
            matmul(left[0], pick(mine, False).reshape(-1, rows), (1, 0))
            + matmul(left[1], pick(other, False).reshape(-1, rows), (1, 0))
        )
        from_first = jnp.concatenate([inverses[0], cross.astype(BF16)], axis=0)
        from_second = jnp.concatenate([jnp.zeros_like(inverses[1]), inverses[1]], axis=0)
        weights_mine = jnp.where(core == 0, from_first, from_second)
        weights_other = jnp.where(core == 0, from_second, from_first)

        earlier, weights_mine, weights_other = lax.optimization_barrier((earlier, weights_mine, weights_other))

        terms = matmul(factor_panel.reshape(blocks * rows, depth), earlier, (1, 1))
        terms = terms.reshape(blocks, rows, -1)
        kept = jnp.where(core == 0, terms[0], terms[1])
        sent = jnp.where(core == 0, terms[1], terms[0]).astype(BF16)
        kept = (kept + swap_cores(sent).astype(F32)).astype(BF16)
        prefix = sum_rows(kept, "z", n_z)
        part = rows // n_z
        right = jnp.where(core == 0, right_side[0], right_side[1])
        right = lax.dynamic_slice_in_dim(right, z * part, part, axis=0)
        residual = (right.astype(F32) - prefix).astype(BF16)
        residual = spread(residual, "z", n_z).reshape(rows, -1)
        residual_other = swap_cores(residual)

        out = matmul(weights_mine, residual, (1, 0)) + matmul(weights_other, residual_other, (1, 0))
        out = sum_rows(out.astype(BF16), "row", n_row).astype(BF16)
        return spread(out, "row", n_row).reshape(blocks, own, -1)

    return per_device


def solution(mesh):
    n_row, n_col = mesh.shape["row"], mesh.shape["col"]
    n_z = n_col // 2
    split = Mesh(mesh.devices.reshape(n_row, n_z, 2), ("row", "z", "core"))
    col = ("z", "core")
    return jax.shard_map(
        make_per_device(n_row, n_z),
        mesh=split,
        in_specs=(
            P(None, "row", col),
            P("row", col),
            P(None, "row", None),
            P("row", col),
            P(None, col, "row"),
        ),
        out_specs=P(None, col, None),
        check_vma=False,
    )
```

```python
import jax
import jax.numpy as jnp
from jax import lax
from jax.sharding import Mesh, PartitionSpec as P

BF16 = jnp.bfloat16
F32 = jnp.float32
ROW = ("y", "x")


def spread(block, axis, size):
    copies = jnp.broadcast_to(block[None], (size,) + block.shape)
    return lax.all_to_all(copies, axis, 0, 0)


def sum_rows(terms, axis, size):
    rows, cols = terms.shape
    pieces = lax.all_to_all(terms.reshape(size, rows // size, cols), axis, 0, 0)
    return jnp.sum(pieces.astype(F32), axis=0)


def swap_cores(block):
    return lax.ppermute(block, "core", [(0, 1), (1, 0)])


def matmul(a, b, contract):
    return lax.dot_general(a, b, ((contract[0:1], contract[1:2]), ((), ())), preferred_element_type=F32)


def make_per_device(n_row, n_x, n_z):
    def per_device(factor_panel, solved_earlier, right_side, coupling, inverses):
        core = lax.axis_index("core")
        z = lax.axis_index("z")
        blocks, rows, depth = factor_panel.shape
        own = coupling.shape[1]

        earlier = lax.all_gather(solved_earlier, ROW, axis=0, tiled=True)

        packed = jnp.concatenate([coupling.T, inverses[0]], axis=0)
        mine = spread(packed, "z", n_z)
        other = swap_cores(mine)

        def pick(part, first):
            return part[:, :own] if first else part[:, own:]

        left = [
            matmul(inverses[1], pick(part, True).reshape(-1, rows), (1, 1)).astype(BF16)
            for part in (mine, other)
        ]
        left = sum_rows(jnp.concatenate(left, axis=0), "x", n_x).astype(BF16)
        earlier, left = lax.optimization_barrier((earlier, left))
        quarters = lax.all_gather(left, ROW, axis=0, tiled=False)
        quarters = quarters.reshape(n_row // n_x, n_x * left.shape[0], -1)
        left = jnp.sum(quarters.astype(F32), axis=0).astype(BF16).reshape(2, own, -1)
        cross = -(
            matmul(left[0], pick(mine, False).reshape(-1, rows), (1, 0))
            + matmul(left[1], pick(other, False).reshape(-1, rows), (1, 0))
        )
        from_first = jnp.concatenate([inverses[0], cross.astype(BF16)], axis=0)
        from_second = jnp.concatenate([jnp.zeros_like(inverses[1]), inverses[1]], axis=0)
        weights_mine = jnp.where(core == 0, from_first, from_second)
        weights_other = jnp.where(core == 0, from_second, from_first)

        terms = matmul(factor_panel.reshape(blocks * rows, depth), earlier, (1, 1))
        terms = terms.reshape(blocks, rows, -1)
        kept = jnp.where(core == 0, terms[0], terms[1])
        sent = jnp.where(core == 0, terms[1], terms[0]).astype(BF16)
        kept = (kept + swap_cores(sent).astype(F32)).astype(BF16)
        prefix = sum_rows(kept, "z", n_z)
        part = rows // n_z
        right = jnp.where(core == 0, right_side[0], right_side[1])
        right = lax.dynamic_slice_in_dim(right, z * part, part, axis=0)
        residual = (right.astype(F32) - prefix).astype(BF16)
        residual = spread(residual, "z", n_z).reshape(rows, -1)
        residual_other = swap_cores(residual)

        out = matmul(weights_mine, residual, (1, 0)) + matmul(weights_other, residual_other, (1, 0))
        out = sum_rows(out.astype(BF16), ROW, n_row).astype(BF16)
        return spread(out, ROW, n_row).reshape(blocks, own, -1)

    return per_device


def solution(mesh):
    n_row, n_col = mesh.shape["row"], mesh.shape["col"]
    n_z = n_col // 2
    n_x = 4
    split = Mesh(mesh.devices.reshape(n_row // n_x, n_x, n_z, 2), ("y", "x", "z", "core"))
    col = ("z", "core")
    return jax.shard_map(
        make_per_device(n_row, n_x, n_z),
        mesh=split,
        in_specs=(
            P(None, ROW, col),
            P(ROW, col),
            P(None, ROW, None),
            P(ROW, col),
            P(None, col, ROW),
        ),
        out_specs=P(None, col, None),
        check_vma=False,
    )
```

```python
import jax
import jax.numpy as jnp
from jax import lax
from jax.sharding import Mesh, PartitionSpec as P

BF16 = jnp.bfloat16
F32 = jnp.float32
ROW = ("y", "x")
SPLIT = 18


def spread(block, axis, size):
    copies = jnp.broadcast_to(block[None], (size,) + block.shape)
    return lax.all_to_all(copies, axis, 0, 0)


def sum_rows(terms, axis, size):
    rows, cols = terms.shape
    pieces = lax.all_to_all(terms.reshape(size, rows // size, cols), axis, 0, 0)
    return jnp.sum(pieces.astype(F32), axis=0)


def swap_cores(block):
    return lax.ppermute(block, "core", [(0, 1), (1, 0)])


def gather_both_ways(block, n_y, n_x, is_first):
    def place(y, x, core):
        return (y * n_x + x) * 2 + core

    def along_x(core):
        return [[place(y, x, core) for x in range(n_x)] for y in range(n_y)]

    def along_y(core):
        return [[place(y, x, core) for y in range(n_y)] for x in range(n_x)]

    for groups in (along_x(0) + along_y(1), along_y(0) + along_x(1)):
        copies = jnp.broadcast_to(block[None], (len(groups[0]),) + block.shape)
        block = lax.all_to_all(copies, ("y", "x", "core"), 0, 0, axis_index_groups=groups)
    block = jnp.where(is_first, block, jnp.swapaxes(block, 0, 1))
    return block.reshape(-1, block.shape[-1])


def matmul(a, b, contract):
    return lax.dot_general(a, b, ((contract[0:1], contract[1:2]), ((), ())), preferred_element_type=F32)


def make_per_device(n_row, n_y, n_x, n_z):
    def per_device(factor_panel, solved_earlier, right_side, coupling, inverses):
        core = lax.axis_index("core")
        z = lax.axis_index("z")
        _, rows, _ = factor_panel.shape
        own = coupling.shape[1]
        part = rows // n_z
        is_first = core == 0

        depth = solved_earlier.shape[1]
        split = depth * SPLIT // 24
        earlier = lax.all_gather(solved_earlier[:, :split], ROW, axis=0, tiled=True)

        right = jnp.where(is_first, right_side[0], right_side[1])
        right = lax.dynamic_slice_in_dim(right, z * part, part, axis=0)
        packed = jnp.concatenate([coupling.T, inverses[0]], axis=0)
        rest = gather_both_ways(solved_earlier[:, split:], n_y, n_x, core == 0)
        packed, right, is_first, rest = lax.optimization_barrier((packed, right, is_first, rest))

        mine = spread(packed, "z", n_z)
        other = swap_cores(mine)
        left = [
            matmul(inverses[1], part_[:, :own].reshape(-1, rows), (1, 1)).astype(BF16)
            for part_ in (mine, other)
        ]
        left = jnp.concatenate(left, axis=0)
        quarters = lax.all_gather(left, ROW, axis=0, tiled=False)
        panel = factor_panel.reshape(2 * rows, depth)
        rest = matmul(panel[:, split:], rest, (1, 1))
        earlier, _, rest = lax.optimization_barrier((earlier, left, rest))

        terms = (rest + matmul(panel[:, :split], earlier, (1, 1))).reshape(2, rows, -1)
        kept = jnp.where(is_first, terms[0], terms[1])
        sent = jnp.where(is_first, terms[1], terms[0]).astype(BF16)
        kept = (kept + swap_cores(sent).astype(F32)).astype(BF16)
        prefix = sum_rows(kept, "z", n_z)
        residual = (right.astype(F32) - prefix).astype(BF16)
        residual = spread(residual, "z", n_z).reshape(rows, -1)
        residual_other = swap_cores(residual)

        _, quarters = lax.optimization_barrier((residual, quarters))
        left = jnp.sum(quarters.astype(F32), axis=0).astype(BF16).reshape(2, own, -1)
        cross = -(
            matmul(left[0], mine[:, own:].reshape(-1, rows), (1, 0))
            + matmul(left[1], other[:, own:].reshape(-1, rows), (1, 0))
        )
        from_first = jnp.concatenate([inverses[0], cross.astype(BF16)], axis=0)
        from_second = jnp.concatenate([jnp.zeros_like(inverses[1]), inverses[1]], axis=0)
        weights_mine = jnp.where(is_first, from_first, from_second)
        weights_other = jnp.where(is_first, from_second, from_first)
        out = matmul(weights_mine, residual, (1, 0)) + matmul(weights_other, residual_other, (1, 0))
        out = sum_rows(out.astype(BF16), ROW, n_row).astype(BF16)
        return spread(out, ROW, n_row).reshape(2, own, -1)

    return per_device


def solution(mesh):
    n_row, n_col = mesh.shape["row"], mesh.shape["col"]
    n_x = 4
    n_y = n_row // n_x
    n_z = n_col // 2
    split = Mesh(mesh.devices.reshape(n_y, n_x, n_z, 2), ("y", "x", "z", "core"))
    col = ("z", "core")
    return jax.shard_map(
        make_per_device(n_row, n_y, n_x, n_z),
        mesh=split,
        in_specs=(
            P(None, ROW, col),
            P(ROW, col),
            P(None, ROW, None),
            P(ROW, col),
            P(None, col, ROW),
        ),
        out_specs=P(None, col, None),
        check_vma=False,
    )
```

```python
import jax
import jax.numpy as jnp
from jax import lax
from jax.sharding import Mesh, PartitionSpec as P

BF16 = jnp.bfloat16
F32 = jnp.float32
ROW = ("y", "x")
COL = ("z", "core")
PLANE = ("y", "x", "core")


def spread(block, axis, size, groups=None):
    copies = jnp.broadcast_to(block[None], (size,) + block.shape)
    return lax.all_to_all(copies, axis, 0, 0, axis_index_groups=groups)


def gather_both_ways(block, n_y, n_x):
    def place(y, x, core):
        return (y * n_x + x) * 2 + core

    def along_x(core):
        return [[place(y, x, core) for x in range(n_x)] for y in range(n_y)]

    def along_y(core):
        return [[place(y, x, core) for y in range(n_y)] for x in range(n_x)]

    for groups in (along_x(0) + along_y(1), along_y(0) + along_x(1)):
        block = spread(block, PLANE, n_x, groups)
    return block


def swap_cores(block):
    return lax.ppermute(block, "core", [(0, 1), (1, 0)])


def times_transposed(a, b):
    return lax.dot_general(a, b, (((1,), (1,)), ((), ())), preferred_element_type=F32)


def make_per_device(n_y, n_x, n_z):
    n_row = n_y * n_x

    def per_device(factor_panel, solved_earlier, right_side, coupling, inverses):
        core = lax.axis_index("core")
        z = lax.axis_index("z")
        is_first = core == 0
        blocks, rows, depth = factor_panel.shape
        rhs = right_side.shape[2]
        own = coupling.shape[1]
        step = 2 * own // n_row
        width = rhs // (2 * n_z)

        packed = jnp.concatenate([coupling.T, inverses[0], inverses[1]], axis=0)
        factors = lax.all_gather(packed, COL, axis=0, tiled=False)

        wanted = core * (rhs // 2) + z * width + lax.broadcasted_iota(jnp.int32, (width, rhs), 0)
        pick = (wanted == lax.broadcasted_iota(jnp.int32, (width, rhs), 1)).astype(BF16)
        right = times_transposed(pick, right_side.reshape(blocks * rows, rhs))

        def gather(block):
            return gather_both_ways(block, n_y, n_x)

        def gather_halves(block):
            return jnp.concatenate([gather(half_) for half_ in jnp.split(block, 2, axis=1)], axis=-1)

        earlier = lax.cond(z < n_z, gather, gather_halves, solved_earlier).reshape(-1, depth)
        earlier, right, is_first = lax.optimization_barrier((earlier, right, is_first))

        terms = times_transposed(earlier, factor_panel.reshape(blocks * rows, depth))
        terms = terms.reshape(n_y, n_x, -1, blocks * rows)
        turned = jnp.swapaxes(terms, 0, 1)
        half = n_y // 2
        kept = jnp.where(is_first, terms[:half], turned[half:])
        sent = jnp.where(is_first, terms[half:], turned[:half]).astype(BF16)
        kept = (kept + swap_cores(sent).astype(F32)).astype(BF16)
        prefix = lax.all_to_all(kept.reshape(n_z, width, blocks * rows), "z", 0, 0)
        prefix, factors = lax.optimization_barrier((prefix, factors))
        prefix = jnp.sum(prefix.astype(F32), axis=0)

        factors = factors.reshape(n_z, 2, 3, n_row // 2, step, rows)
        factors = factors.transpose(2, 1, 3, 0, 4, 5).reshape(3, n_row * n_z * step, rows)

        def solve(residual, inverse):
            terms = times_transposed(residual, inverse).astype(BF16)
            terms = terms.reshape(width, n_row, -1).transpose(1, 0, 2)
            terms = lax.all_to_all(terms, ROW, 0, 0)
            return jnp.sum(terms.astype(F32), axis=0).astype(BF16)

        residual_first = (right[:, :rows] - prefix[:, :rows]).astype(BF16)
        first = solve(residual_first, factors[1])
        all_first = spread(first, ROW, n_row).transpose(1, 0, 2).reshape(width, -1)
        cross = jnp.dot(all_first, factors[0], preferred_element_type=F32)
        residual_second = (right[:, rows:] - (prefix[:, rows:] + cross)).astype(BF16)
        second = solve(residual_second, factors[2])

        solved = jnp.stack([first.T, second.T]).reshape(2, n_z, step, width)
        solved = solved.transpose(1, 0, 2, 3).reshape(n_z, 2 * step, width)
        solved = lax.all_to_all(solved, "z", 0, 0)
        solved = solved.transpose(1, 0, 2).reshape(2 * step, rhs // 2)
        solved = spread(solved, PLANE, 2 * n_row)
        solved = solved.reshape(2, n_row // 2, 2, 2, step, rhs // 2)
        solved = jnp.where(is_first, solved[0], solved[1])
        return solved.transpose(2, 0, 3, 1, 4).reshape(2, own, rhs)

    return per_device


def solution(mesh):
    n_row, n_col = mesh.shape["row"], mesh.shape["col"]
    n_x = 4
    n_y = n_row // n_x
    n_z = n_col // 2
    split = Mesh(mesh.devices.reshape(n_y, n_x, n_z, 2), ("y", "x", "z", "core"))
    return jax.shard_map(
        make_per_device(n_y, n_x, n_z),
        mesh=split,
        in_specs=(
            P(None, ROW, COL),
            P(ROW, COL),
            P(None, ROW, None),
            P(ROW, COL),
            P(None, COL, ROW),
        ),
        out_specs=P(None, COL, None),
        check_vma=False,
    )
```

```python
import jax
import jax.numpy as jnp
from jax import lax
from jax.experimental import pallas as pl
from jax.experimental.pallas import tpu as pltpu
from jax.sharding import Mesh, PartitionSpec as P

BF16 = jnp.bfloat16
F32 = jnp.float32
ROW = ("y", "x")
SPLIT = 20


def spread(block, axis, size):
    copies = jnp.broadcast_to(block[None], (size,) + block.shape)
    return lax.all_to_all(copies, axis, 0, 0)


def sum_rows(terms, axis, size):
    rows, cols = terms.shape
    pieces = lax.all_to_all(terms.reshape(size, rows // size, cols), axis, 0, 0)
    return jnp.sum(pieces.astype(F32), axis=0)


def swap_cores(block):
    return lax.ppermute(block, "core", [(0, 1), (1, 0)])


def gather_both_ways(block, n_y, n_x, is_first):
    def place(y, x, core):
        return (y * n_x + x) * 2 + core

    def along_x(core):
        return [[place(y, x, core) for x in range(n_x)] for y in range(n_y)]

    def along_y(core):
        return [[place(y, x, core) for y in range(n_y)] for x in range(n_x)]

    for groups in (along_x(0) + along_y(1), along_y(0) + along_x(1)):
        copies = jnp.broadcast_to(block[None], (len(groups[0]),) + block.shape)
        block = lax.all_to_all(copies, ("y", "x", "core"), 0, 0, axis_index_groups=groups)
    block = jnp.where(is_first, block, jnp.swapaxes(block, 0, 1))
    return block.reshape(-1, block.shape[-1])


def matmul(a, b, contract):
    return lax.dot_general(a, b, ((contract[0:1], contract[1:2]), ((), ())), preferred_element_type=F32)


def add_terms(terms_ref, out_ref, total_ref):
    @pl.when(pl.program_id(0) == 0)
    def _():
        total_ref[...] = jnp.zeros_like(total_ref)

    total = total_ref[...]
    for i in range(terms_ref.shape[0]):
        total += terms_ref[i].astype(F32)
    total_ref[...] = total

    @pl.when(pl.program_id(0) == pl.num_programs(0) - 1)
    def _():
        out_ref[...] = total_ref[...].astype(BF16)


def sum_terms(terms, at_once):
    count, rows, cols = terms.shape
    return pl.pallas_call(
        add_terms,
        grid=(count // at_once,),
        in_specs=[pl.BlockSpec((at_once, rows, cols), lambda i: (i, 0, 0))],
        out_specs=pl.BlockSpec((rows, cols), lambda i: (0, 0)),
        out_shape=jax.ShapeDtypeStruct((rows, cols), BF16),
        scratch_shapes=[pltpu.VMEM((rows, cols), F32)],
        compiler_params=pltpu.CompilerParams(vmem_limit_bytes=32 * 2**20),
        cost_estimate=pl.CostEstimate(
            flops=count * rows * cols, bytes_accessed=2 * (count + 1) * rows * cols, transcendentals=0
        ),
    )(terms)


def make_per_device(n_row, n_y, n_x, n_z):
    def per_device(factor_panel, solved_earlier, right_side, coupling, inverses):
        core = lax.axis_index("core")
        z = lax.axis_index("z")
        _, rows, _ = factor_panel.shape
        own = coupling.shape[1]
        part = rows // n_z
        is_first = core == 0

        depth = solved_earlier.shape[1]
        split = depth * SPLIT // 24
        earlier = lax.all_gather(solved_earlier[:, :split], ROW, axis=0, tiled=True)

        right = jnp.where(is_first, right_side[0], right_side[1])
        right = lax.dynamic_slice_in_dim(right, z * part, part, axis=0)
        packed = jnp.concatenate([coupling.T, inverses[0]], axis=0)
        rest = gather_both_ways(solved_earlier[:, split:], n_y, n_x, core == 0)
        packed, right, is_first, rest = lax.optimization_barrier((packed, right, is_first, rest))

        mine = spread(packed, "z", n_z)
        other = swap_cores(mine)
        left = [
            matmul(inverses[1], part_[:, :own].reshape(-1, rows), (1, 1)).astype(BF16)
            for part_ in (mine, other)
        ]
        even = lax.axis_index("x") % 2 == 0
        pairs = [(x, x ^ 1) for x in range(n_x)]
        received = lax.ppermute(jnp.where(even, left[1], left[0]), "x", pairs)
        left = (jnp.where(even, left[0], left[1]).astype(F32) + received.astype(F32)).astype(BF16)
        quarters = lax.all_gather(left, ROW, axis=0, tiled=False)
        panel = factor_panel.reshape(2 * rows, depth)
        rest = matmul(panel[:, split:], rest, (1, 1))
        earlier, _, rest = lax.optimization_barrier((earlier, left, rest))

        terms = (rest + matmul(panel[:, :split], earlier, (1, 1))).reshape(2, rows, -1)
        kept = jnp.where(is_first, terms[0], terms[1])
        sent = jnp.where(is_first, terms[1], terms[0]).astype(BF16)
        kept = (kept + swap_cores(sent).astype(F32)).astype(BF16)
        prefix = sum_rows(kept, "z", n_z)
        residual = (right.astype(F32) - prefix).astype(BF16)
        residual = spread(residual, "z", n_z).reshape(rows, -1)
        residual_other = swap_cores(residual)

        _, quarters = lax.optimization_barrier((residual, quarters))
        left = sum_terms(quarters.reshape(n_row // 2, 2 * own, -1), 4).reshape(2, own, -1)
        cross = -(
            matmul(left[0], mine[:, own:].reshape(-1, rows), (1, 0))
            + matmul(left[1], other[:, own:].reshape(-1, rows), (1, 0))
        )
        from_first = jnp.concatenate([inverses[0], cross.astype(BF16)], axis=0)
        from_second = jnp.concatenate([jnp.zeros_like(inverses[1]), inverses[1]], axis=0)
        weights_mine = jnp.where(is_first, from_first, from_second)
        weights_other = jnp.where(is_first, from_second, from_first)
        out = matmul(weights_mine, residual, (1, 0)) + matmul(weights_other, residual_other, (1, 0))
        out = sum_rows(out.astype(BF16), ROW, n_row).astype(BF16)
        return spread(out, ROW, n_row).reshape(2, own, -1)

    return per_device


def solution(mesh):
    n_row, n_col = mesh.shape["row"], mesh.shape["col"]
    n_x = 4
    n_y = n_row // n_x
    n_z = n_col // 2
    split = Mesh(mesh.devices.reshape(n_y, n_x, n_z, 2), ("y", "x", "z", "core"))
    col = ("z", "core")
    return jax.shard_map(
        make_per_device(n_row, n_y, n_x, n_z),
        mesh=split,
        in_specs=(
            P(None, ROW, col),
            P(ROW, col),
            P(None, ROW, None),
            P(ROW, col),
            P(None, col, ROW),
        ),
        out_specs=P(None, col, None),
        check_vma=False,
    )
```

```python
import jax
import jax.numpy as jnp
from jax import lax
from jax.experimental import pallas as pl
from jax.experimental.pallas import tpu as pltpu
from jax.sharding import Mesh, PartitionSpec as P

BF16 = jnp.bfloat16
F32 = jnp.float32
ROW = ("y", "x")
SPLIT = 20


def spread(block, axis, size):
    copies = jnp.broadcast_to(block[None], (size,) + block.shape)
    return lax.all_to_all(copies, axis, 0, 0)


def sum_rows(terms, axis, size):
    rows, cols = terms.shape
    pieces = lax.all_to_all(terms.reshape(size, rows // size, cols), axis, 0, 0)
    return jnp.sum(pieces.astype(F32), axis=0)


def swap_cores(block):
    return lax.ppermute(block, "core", [(0, 1), (1, 0)])


def gather_both_ways(block, n_y, n_x, is_first):
    def place(y, x, core):
        return (y * n_x + x) * 2 + core

    def along_x(core):
        return [[place(y, x, core) for x in range(n_x)] for y in range(n_y)]

    def along_y(core):
        return [[place(y, x, core) for y in range(n_y)] for x in range(n_x)]

    for groups in (along_x(0) + along_y(1), along_y(0) + along_x(1)):
        copies = jnp.broadcast_to(block[None], (len(groups[0]),) + block.shape)
        block = lax.all_to_all(copies, ("y", "x", "core"), 0, 0, axis_index_groups=groups)
    block = jnp.where(is_first, block, jnp.swapaxes(block, 0, 1))
    return block.reshape(-1, block.shape[-1])


def matmul(a, b, contract):
    return lax.dot_general(a, b, ((contract[0:1], contract[1:2]), ((), ())), preferred_element_type=F32)


def add_terms(terms_ref, out_ref, total_ref):
    @pl.when(pl.program_id(0) == 0)
    def _():
        total_ref[...] = jnp.zeros_like(total_ref)

    total = total_ref[...]
    for i in range(terms_ref.shape[0]):
        total += terms_ref[i].astype(F32)
    total_ref[...] = total

    @pl.when(pl.program_id(0) == pl.num_programs(0) - 1)
    def _():
        out_ref[...] = total_ref[...].astype(BF16)


def sum_terms(terms, at_once):
    count, rows, cols = terms.shape
    return pl.pallas_call(
        add_terms,
        grid=(count // at_once,),
        in_specs=[pl.BlockSpec((at_once, rows, cols), lambda i: (i, 0, 0))],
        out_specs=pl.BlockSpec((rows, cols), lambda i: (0, 0)),
        out_shape=jax.ShapeDtypeStruct((rows, cols), BF16),
        scratch_shapes=[pltpu.VMEM((rows, cols), F32)],
        compiler_params=pltpu.CompilerParams(vmem_limit_bytes=32 * 2**20),
        cost_estimate=pl.CostEstimate(
            flops=count * rows * cols, bytes_accessed=2 * (count + 1) * rows * cols, transcendentals=0
        ),
    )(terms)


def make_per_device(n_row, n_y, n_x, n_z):
    def per_device(factor_panel, solved_earlier, right_side, coupling, inverses):
        core = lax.axis_index("core")
        z = lax.axis_index("z")
        _, rows, _ = factor_panel.shape
        own = coupling.shape[1]
        part = rows // n_z
        is_first = core == 0

        depth = solved_earlier.shape[1]
        split = depth * SPLIT // 24
        earlier = lax.all_gather(solved_earlier[:, :split], ROW, axis=0, tiled=True)

        right = jnp.where(is_first, right_side[0], right_side[1])
        right = lax.dynamic_slice_in_dim(right, z * part, part, axis=0)
        packed = jnp.concatenate([coupling.T, inverses[0]], axis=0)
        rest = gather_both_ways(solved_earlier[:, split:], n_y, n_x, core == 0)
        packed, right, is_first, rest = lax.optimization_barrier((packed, right, is_first, rest))

        mine = spread(packed, "z", n_z)
        other = swap_cores(mine)
        left = [
            matmul(inverses[1], part_[:, :own].reshape(-1, rows), (1, 1)).astype(BF16)
            for part_ in (mine, other)
        ]
        even = lax.axis_index("x") % 2 == 0
        pairs = [(x, x ^ 1) for x in range(n_x)]
        received = lax.ppermute(jnp.where(even, left[1], left[0]), "x", pairs)
        panel = factor_panel.reshape(2 * rows, depth)
        rest = matmul(panel[:, split:], rest, (1, 1))
        received, rest = lax.optimization_barrier((received, rest))
        left = (jnp.where(even, left[0], left[1]).astype(F32) + received.astype(F32)).astype(BF16)
        quarters = lax.all_gather(left, ROW, axis=0, tiled=False)
        earlier, _, rest = lax.optimization_barrier((earlier, left, rest))

        terms = (rest + matmul(panel[:, :split], earlier, (1, 1))).reshape(2, rows, -1)
        kept = jnp.where(is_first, terms[0], terms[1])
        sent = jnp.where(is_first, terms[1], terms[0]).astype(BF16)
        kept = (kept + swap_cores(sent).astype(F32)).astype(BF16)
        prefix = sum_rows(kept, "z", n_z)
        residual = (right.astype(F32) - prefix).astype(BF16)
        residual = spread(residual, "z", n_z).reshape(rows, -1)
        residual_other = swap_cores(residual)

        _, quarters = lax.optimization_barrier((residual, quarters))
        left = sum_terms(quarters.reshape(n_row // 2, 2 * own, -1), 4).reshape(2, own, -1)
        cross = -(
            matmul(left[0], mine[:, own:].reshape(-1, rows), (1, 0))
            + matmul(left[1], other[:, own:].reshape(-1, rows), (1, 0))
        )
        from_first = jnp.concatenate([inverses[0], cross.astype(BF16)], axis=0)
        from_second = jnp.concatenate([jnp.zeros_like(inverses[1]), inverses[1]], axis=0)
        weights_mine = jnp.where(is_first, from_first, from_second)
        weights_other = jnp.where(is_first, from_second, from_first)
        out = matmul(weights_mine, residual, (1, 0)) + matmul(weights_other, residual_other, (1, 0))
        out = sum_rows(out.astype(BF16), ROW, n_row).astype(BF16)
        return spread(out, ROW, n_row).reshape(2, own, -1)

    return per_device


def solution(mesh):
    n_row, n_col = mesh.shape["row"], mesh.shape["col"]
    n_x = 4
    n_y = n_row // n_x
    n_z = n_col // 2
    split = Mesh(mesh.devices.reshape(n_y, n_x, n_z, 2), ("y", "x", "z", "core"))
    col = ("z", "core")
    return jax.shard_map(
        make_per_device(n_row, n_y, n_x, n_z),
        mesh=split,
        in_specs=(
            P(None, ROW, col),
            P(ROW, col),
            P(None, ROW, None),
            P(ROW, col),
            P(None, col, ROW),
        ),
        out_specs=P(None, col, None),
        check_vma=False,
    )
```

```python
import jax
import jax.numpy as jnp
from jax import lax
from jax.experimental import pallas as pl
from jax.experimental.pallas import tpu as pltpu
from jax.sharding import Mesh, PartitionSpec as P

BF16 = jnp.bfloat16
F32 = jnp.float32
ROW = ("y", "x")
SPLIT = 21


def spread(block, axis, size):
    copies = jnp.broadcast_to(block[None], (size,) + block.shape)
    return lax.all_to_all(copies, axis, 0, 0)


def sum_rows(terms, axis, size):
    rows, cols = terms.shape
    pieces = lax.all_to_all(terms.reshape(size, rows // size, cols), axis, 0, 0)
    return jnp.sum(pieces.astype(F32), axis=0)


def swap_cores(block):
    return lax.ppermute(block, "core", [(0, 1), (1, 0)])


def gather_both_ways(block, n_y, n_x, is_first):
    def place(y, x, core):
        return (y * n_x + x) * 2 + core

    def along_x(core):
        return [[place(y, x, core) for x in range(n_x)] for y in range(n_y)]

    def along_y(core):
        return [[place(y, x, core) for y in range(n_y)] for x in range(n_x)]

    for groups in (along_x(0) + along_y(1), along_y(0) + along_x(1)):
        copies = jnp.broadcast_to(block[None], (len(groups[0]),) + block.shape)
        block = lax.all_to_all(copies, ("y", "x", "core"), 0, 0, axis_index_groups=groups)
    block = jnp.where(is_first, block, jnp.swapaxes(block, 0, 1))
    return block.reshape(-1, block.shape[-1])


def matmul(a, b, contract):
    return lax.dot_general(a, b, ((contract[0:1], contract[1:2]), ((), ())), preferred_element_type=F32)


def add_terms(terms_ref, out_ref, total_ref):
    @pl.when(pl.program_id(0) == 0)
    def _():
        total_ref[...] = jnp.zeros_like(total_ref)

    total = total_ref[...]
    for i in range(terms_ref.shape[0]):
        total += terms_ref[i].astype(F32)
    total_ref[...] = total

    @pl.when(pl.program_id(0) == pl.num_programs(0) - 1)
    def _():
        out_ref[...] = total_ref[...].astype(BF16)


def sum_terms(terms, at_once):
    count, rows, cols = terms.shape
    return pl.pallas_call(
        add_terms,
        grid=(count // at_once,),
        in_specs=[pl.BlockSpec((at_once, rows, cols), lambda i: (i, 0, 0))],
        out_specs=pl.BlockSpec((rows, cols), lambda i: (0, 0)),
        out_shape=jax.ShapeDtypeStruct((rows, cols), BF16),
        scratch_shapes=[pltpu.VMEM((rows, cols), F32)],
        compiler_params=pltpu.CompilerParams(vmem_limit_bytes=32 * 2**20),
        cost_estimate=pl.CostEstimate(
            flops=count * rows * cols, bytes_accessed=2 * (count + 1) * rows * cols, transcendentals=0
        ),
    )(terms)


def make_per_device(n_row, n_y, n_x, n_z):
    def per_device(factor_panel, solved_earlier, right_side, coupling, inverses):
        core = lax.axis_index("core")
        z = lax.axis_index("z")
        _, rows, _ = factor_panel.shape
        own = coupling.shape[1]
        part = rows // n_z
        is_first = core == 0

        depth = solved_earlier.shape[1]
        split = depth * SPLIT // 24
        earlier = lax.all_gather(solved_earlier[:, :split], ROW, axis=0, tiled=True)

        right = jnp.where(is_first, right_side[0], right_side[1])
        right = lax.dynamic_slice_in_dim(right, z * part, part, axis=0)
        packed = jnp.concatenate([coupling.T, inverses[0]], axis=0)
        rest = gather_both_ways(solved_earlier[:, split:], n_y, n_x, core == 0)
        packed, right, is_first, rest = lax.optimization_barrier((packed, right, is_first, rest))

        mine = spread(packed, "z", n_z)
        other = swap_cores(mine)
        left = [
            matmul(inverses[1], part_[:, :own].reshape(-1, rows), (1, 1)).astype(BF16)
            for part_ in (mine, other)
        ]
        even = lax.axis_index("x") % 2 == 0
        pairs = [(x, x ^ 1) for x in range(n_x)]
        received = lax.ppermute(jnp.where(even, left[1], left[0]), "x", pairs)
        panel = factor_panel.reshape(2 * rows, depth)
        rest = matmul(panel[:, split:], rest, (1, 1))
        received, rest = lax.optimization_barrier((received, rest))
        left = (jnp.where(even, left[0], left[1]).astype(F32) + received.astype(F32)).astype(BF16)
        quarters = lax.all_gather(left, ROW, axis=0, tiled=False)
        earlier, _, rest = lax.optimization_barrier((earlier, left, rest))

        terms = (rest + matmul(panel[:, :split], earlier, (1, 1))).reshape(2, rows, -1)
        kept = jnp.where(is_first, terms[0], terms[1])
        sent = jnp.where(is_first, terms[1], terms[0]).astype(BF16)
        kept = (kept + swap_cores(sent).astype(F32)).astype(BF16)
        prefix = sum_rows(kept, "z", n_z)
        residual = (right.astype(F32) - prefix).astype(BF16)
        residual = spread(residual, "z", n_z).reshape(rows, -1)
        residual_other = swap_cores(residual)

        _, quarters = lax.optimization_barrier((residual, quarters))
        left = sum_terms(quarters.reshape(n_row // 2, 2 * own, -1), 4).reshape(2, own, -1)
        cross = -(
            matmul(left[0], mine[:, own:].reshape(-1, rows), (1, 0))
            + matmul(left[1], other[:, own:].reshape(-1, rows), (1, 0))
        )
        from_first = jnp.concatenate([inverses[0], cross.astype(BF16)], axis=0)
        from_second = jnp.concatenate([jnp.zeros_like(inverses[1]), inverses[1]], axis=0)
        weights_mine = jnp.where(is_first, from_first, from_second)
        weights_other = jnp.where(is_first, from_second, from_first)
        out = matmul(weights_mine, residual, (1, 0)) + matmul(weights_other, residual_other, (1, 0))
        out = sum_rows(out.astype(BF16), ROW, n_row).astype(BF16)
        return spread(out, ROW, n_row).reshape(2, own, -1)

    return per_device


def solution(mesh):
    n_row, n_col = mesh.shape["row"], mesh.shape["col"]
    n_x = 4
    n_y = n_row // n_x
    n_z = n_col // 2
    split = Mesh(mesh.devices.reshape(n_y, n_x, n_z, 2), ("y", "x", "z", "core"))
    col = ("z", "core")
    return jax.shard_map(
        make_per_device(n_row, n_y, n_x, n_z),
        mesh=split,
        in_specs=(
            P(None, ROW, col),
            P(ROW, col),
            P(None, ROW, None),
            P(ROW, col),
            P(None, col, ROW),
        ),
        out_specs=P(None, col, None),
        check_vma=False,
    )
```

```python
import jax
import jax.numpy as jnp
from jax import lax
from jax.experimental import pallas as pl
from jax.experimental.pallas import tpu as pltpu
from jax.sharding import Mesh, PartitionSpec as P

BF16 = jnp.bfloat16
F32 = jnp.float32
ROW = ("y", "x")
Z = ("far", "near")
SPLIT = 20


def spread(block, axis, size):
    copies = jnp.broadcast_to(block[None], (size,) + block.shape)
    return lax.all_to_all(copies, axis, 0, 0)


def sum_rows(terms, axis, size):
    rows, cols = terms.shape
    pieces = lax.all_to_all(terms.reshape(size, rows // size, cols), axis, 0, 0)
    return jnp.sum(pieces.astype(F32), axis=0)


def swap_cores(block):
    return lax.ppermute(block, "core", [(0, 1), (1, 0)])


def gather_both_ways(block, n_y, n_x, is_first):
    def place(y, x, core):
        return (y * n_x + x) * 2 + core

    def along_x(core):
        return [[place(y, x, core) for x in range(n_x)] for y in range(n_y)]

    def along_y(core):
        return [[place(y, x, core) for y in range(n_y)] for x in range(n_x)]

    for groups in (along_x(0) + along_y(1), along_y(0) + along_x(1)):
        copies = jnp.broadcast_to(block[None], (len(groups[0]),) + block.shape)
        block = lax.all_to_all(copies, ("y", "x", "core"), 0, 0, axis_index_groups=groups)
    block = jnp.where(is_first, block, jnp.swapaxes(block, 0, 1))
    return block.reshape(-1, block.shape[-1])


def matmul(a, b, contract):
    return lax.dot_general(a, b, ((contract[0:1], contract[1:2]), ((), ())), preferred_element_type=F32)


def add_terms(terms_ref, out_ref, total_ref):
    @pl.when(pl.program_id(0) == 0)
    def _():
        total_ref[...] = jnp.zeros_like(total_ref)

    total = total_ref[...]
    for i in range(terms_ref.shape[0]):
        total += terms_ref[i].astype(F32)
    total_ref[...] = total

    @pl.when(pl.program_id(0) == pl.num_programs(0) - 1)
    def _():
        out_ref[...] = total_ref[...].astype(BF16)


def sum_terms(terms, at_once):
    count, rows, cols = terms.shape
    return pl.pallas_call(
        add_terms,
        grid=(count // at_once,),
        in_specs=[pl.BlockSpec((at_once, rows, cols), lambda i: (i, 0, 0))],
        out_specs=pl.BlockSpec((rows, cols), lambda i: (0, 0)),
        out_shape=jax.ShapeDtypeStruct((rows, cols), BF16),
        scratch_shapes=[pltpu.VMEM((rows, cols), F32)],
        compiler_params=pltpu.CompilerParams(vmem_limit_bytes=32 * 2**20),
        cost_estimate=pl.CostEstimate(
            flops=count * rows * cols, bytes_accessed=2 * (count + 1) * rows * cols, transcendentals=0
        ),
    )(terms)


def make_per_device(n_row, n_y, n_x, n_z, n_near):
    def per_device(factor_panel, solved_earlier, right_side, coupling, inverses):
        core = lax.axis_index("core")
        near = lax.axis_index("near")
        _, rows, _ = factor_panel.shape
        own = coupling.shape[1]
        part = rows // n_near
        is_first = core == 0

        depth = solved_earlier.shape[1]
        split = depth * SPLIT // 24
        earlier = lax.all_gather(solved_earlier[:, :split], ROW, axis=0, tiled=True)

        right = jnp.where(is_first, right_side[0], right_side[1])
        right = lax.dynamic_slice_in_dim(right, near * part, part, axis=0)
        packed = jnp.concatenate([coupling.T, inverses[0]], axis=0)
        rest = gather_both_ways(solved_earlier[:, split:], n_y, n_x, core == 0)
        packed, right, is_first, rest = lax.optimization_barrier((packed, right, is_first, rest))

        mine = spread(packed, Z, n_z)
        other = swap_cores(mine)
        left = [
            matmul(inverses[1], part_[:, :own].reshape(-1, rows), (1, 1)).astype(BF16)
            for part_ in (mine, other)
        ]
        even = lax.axis_index("x") % 2 == 0
        pairs = [(x, x ^ 1) for x in range(n_x)]
        received = lax.ppermute(jnp.where(even, left[1], left[0]), "x", pairs)
        left = (jnp.where(even, left[0], left[1]).astype(F32) + received.astype(F32)).astype(BF16)
        quarters = lax.all_gather(left, ROW, axis=0, tiled=False)
        panel = factor_panel.reshape(2 * rows, depth)
        rest = matmul(panel[:, split:], rest, (1, 1))
        earlier, _, rest = lax.optimization_barrier((earlier, left, rest))

        terms = (rest + matmul(panel[:, :split], earlier, (1, 1))).reshape(2, rows, -1)
        kept = jnp.where(is_first, terms[0], terms[1])
        sent = jnp.where(is_first, terms[1], terms[0]).astype(BF16)
        kept = (kept + swap_cores(sent).astype(F32)).astype(BF16)
        quarter = sum_rows(kept, "near", n_near).astype(BF16)
        prefix = jnp.sum(spread(quarter, "far", n_z // n_near).astype(F32), axis=0)
        residual = (right.astype(F32) - prefix).astype(BF16)
        residual = spread(residual, "near", n_near).reshape(rows, -1)
        residual_other = swap_cores(residual)

        _, quarters = lax.optimization_barrier((residual, quarters))
        left = sum_terms(quarters.reshape(n_row // 2, 2 * own, -1), 4).reshape(2, own, -1)
        cross = -(
            matmul(left[0], mine[:, own:].reshape(-1, rows), (1, 0))
            + matmul(left[1], other[:, own:].reshape(-1, rows), (1, 0))
        )
        from_first = jnp.concatenate([inverses[0], cross.astype(BF16)], axis=0)
        from_second = jnp.concatenate([jnp.zeros_like(inverses[1]), inverses[1]], axis=0)
        weights_mine = jnp.where(is_first, from_first, from_second)
        weights_other = jnp.where(is_first, from_second, from_first)
        out = matmul(weights_mine, residual, (1, 0)) + matmul(weights_other, residual_other, (1, 0))
        out = sum_rows(out.astype(BF16), ROW, n_row).astype(BF16)
        return spread(out, ROW, n_row).reshape(2, own, -1)

    return per_device


def solution(mesh):
    n_row, n_col = mesh.shape["row"], mesh.shape["col"]
    n_x = 4
    n_y = n_row // n_x
    n_z = n_col // 2
    n_near = 4
    split = Mesh(mesh.devices.reshape(n_y, n_x, n_z // n_near, n_near, 2), ("y", "x", "far", "near", "core"))
    col = ("far", "near", "core")
    return jax.shard_map(
        make_per_device(n_row, n_y, n_x, n_z, n_near),
        mesh=split,
        in_specs=(
            P(None, ROW, col),
            P(ROW, col),
            P(None, ROW, None),
            P(ROW, col),
            P(None, col, ROW),
        ),
        out_specs=P(None, col, None),
        check_vma=False,
    )
```

```python
import jax
import jax.numpy as jnp
from jax import lax
from jax.experimental import pallas as pl
from jax.experimental.pallas import tpu as pltpu
from jax.sharding import Mesh, PartitionSpec as P

BF16 = jnp.bfloat16
F32 = jnp.float32
ROW = ("y", "x")
SPLIT = 20


def spread(block, axis, size):
    copies = jnp.broadcast_to(block[None], (size,) + block.shape)
    return lax.all_to_all(copies, axis, 0, 0)


def sum_rows(terms, axis, size):
    rows, cols = terms.shape
    pieces = lax.all_to_all(terms.reshape(size, rows // size, cols), axis, 0, 0)
    return jnp.sum(pieces.astype(F32), axis=0)


def swap_cores(block):
    return lax.ppermute(block, "core", [(0, 1), (1, 0)])


def gather_both_ways(block, n_y, n_x, is_first):
    def place(y, x, core):
        return (y * n_x + x) * 2 + core

    def along_x(core):
        return [[place(y, x, core) for x in range(n_x)] for y in range(n_y)]

    def along_y(core):
        return [[place(y, x, core) for y in range(n_y)] for x in range(n_x)]

    for groups in (along_x(0) + along_y(1), along_y(0) + along_x(1)):
        copies = jnp.broadcast_to(block[None], (len(groups[0]),) + block.shape)
        block = lax.all_to_all(copies, ("y", "x", "core"), 0, 0, axis_index_groups=groups)
    block = jnp.where(is_first, block, jnp.swapaxes(block, 0, 1))
    return block.reshape(-1, block.shape[-1])


def matmul(a, b, contract):
    return lax.dot_general(a, b, ((contract[0:1], contract[1:2]), ((), ())), preferred_element_type=F32)


def add_terms(terms_ref, out_ref, total_ref):
    @pl.when(pl.program_id(0) == 0)
    def _():
        total_ref[...] = jnp.zeros_like(total_ref)

    total = total_ref[...]
    for i in range(terms_ref.shape[0]):
        total += terms_ref[i].astype(F32)
    total_ref[...] = total

    @pl.when(pl.program_id(0) == pl.num_programs(0) - 1)
    def _():
        out_ref[...] = total_ref[...].astype(BF16)


def sum_terms(terms, at_once):
    count, rows, cols = terms.shape
    return pl.pallas_call(
        add_terms,
        grid=(count // at_once,),
        in_specs=[pl.BlockSpec((at_once, rows, cols), lambda i: (i, 0, 0))],
        out_specs=pl.BlockSpec((rows, cols), lambda i: (0, 0)),
        out_shape=jax.ShapeDtypeStruct((rows, cols), BF16),
        scratch_shapes=[pltpu.VMEM((rows, cols), F32)],
        compiler_params=pltpu.CompilerParams(vmem_limit_bytes=32 * 2**20),
        cost_estimate=pl.CostEstimate(
            flops=count * rows * cols, bytes_accessed=2 * (count + 1) * rows * cols, transcendentals=0
        ),
    )(terms)


def make_per_device(n_row, n_y, n_x, n_z, n_near):
    def per_device(factor_panel, solved_earlier, right_side, coupling, inverses):
        core = lax.axis_index("core")
        near = lax.axis_index("near")
        _, rows, _ = factor_panel.shape
        own = coupling.shape[1]
        part = rows // n_near
        is_first = core == 0

        depth = solved_earlier.shape[1]
        split = depth * SPLIT // 24
        earlier = lax.all_gather(solved_earlier[:, :split], ROW, axis=0, tiled=True)

        right = jnp.where(is_first, right_side[0], right_side[1])
        right = lax.dynamic_slice_in_dim(right, near * part, part, axis=0)
        packed = jnp.concatenate([coupling.T, inverses[0]], axis=0)
        rest = gather_both_ways(solved_earlier[:, split:], n_y, n_x, core == 0)
        packed, right, is_first, rest = lax.optimization_barrier((packed, right, is_first, rest))

        mine = spread(spread(packed, "far", n_z // n_near), "near", n_near).reshape(n_z, *packed.shape)
        other = swap_cores(mine)
        left = [
            matmul(inverses[1], part_[:, :own].reshape(-1, rows), (1, 1)).astype(BF16)
            for part_ in (mine, other)
        ]
        even = lax.axis_index("x") % 2 == 0
        pairs = [(x, x ^ 1) for x in range(n_x)]
        received = lax.ppermute(jnp.where(even, left[1], left[0]), "x", pairs)
        left = (jnp.where(even, left[0], left[1]).astype(F32) + received.astype(F32)).astype(BF16)
        quarters = lax.all_gather(left, ROW, axis=0, tiled=False)
        panel = factor_panel.reshape(2 * rows, depth)
        rest = matmul(panel[:, split:], rest, (1, 1))
        earlier, _, rest = lax.optimization_barrier((earlier, left, rest))

        terms = (rest + matmul(panel[:, :split], earlier, (1, 1))).reshape(2, rows, -1)
        kept = jnp.where(is_first, terms[0], terms[1])
        sent = jnp.where(is_first, terms[1], terms[0]).astype(BF16)
        kept = (kept + swap_cores(sent).astype(F32)).astype(BF16)
        quarter = sum_rows(kept, "near", n_near).astype(BF16)
        prefix = jnp.sum(spread(quarter, "far", n_z // n_near).astype(F32), axis=0)
        residual = (right.astype(F32) - prefix).astype(BF16)
        residual = spread(residual, "near", n_near).reshape(rows, -1)
        residual_other = swap_cores(residual)

        _, quarters = lax.optimization_barrier((residual, quarters))
        left = sum_terms(quarters.reshape(n_row // 2, 2 * own, -1), 4).reshape(2, own, -1)
        cross = -(
            matmul(left[0], mine[:, own:].reshape(-1, rows), (1, 0))
            + matmul(left[1], other[:, own:].reshape(-1, rows), (1, 0))
        )
        from_first = jnp.concatenate([inverses[0], cross.astype(BF16)], axis=0)
        from_second = jnp.concatenate([jnp.zeros_like(inverses[1]), inverses[1]], axis=0)
        weights_mine = jnp.where(is_first, from_first, from_second)
        weights_other = jnp.where(is_first, from_second, from_first)
        out = matmul(weights_mine, residual, (1, 0)) + matmul(weights_other, residual_other, (1, 0))
        out = sum_rows(out.astype(BF16), ROW, n_row).astype(BF16)
        return spread(out, ROW, n_row).reshape(2, own, -1)

    return per_device


def solution(mesh):
    n_row, n_col = mesh.shape["row"], mesh.shape["col"]
    n_x = 4
    n_y = n_row // n_x
    n_z = n_col // 2
    n_near = 4
    split = Mesh(mesh.devices.reshape(n_y, n_x, n_z // n_near, n_near, 2), ("y", "x", "far", "near", "core"))
    col = ("far", "near", "core")
    return jax.shard_map(
        make_per_device(n_row, n_y, n_x, n_z, n_near),
        mesh=split,
        in_specs=(
            P(None, ROW, col),
            P(ROW, col),
            P(None, ROW, None),
            P(ROW, col),
            P(None, col, ROW),
        ),
        out_specs=P(None, col, None),
        check_vma=False,
    )
```

```python
import jax
import jax.numpy as jnp
from jax import lax
from jax.experimental import pallas as pl
from jax.experimental.pallas import tpu as pltpu
from jax.sharding import Mesh, PartitionSpec as P

BF16 = jnp.bfloat16
F32 = jnp.float32
ROW = ("y", "x")
SPLIT = 22


def spread(block, axis, size):
    copies = jnp.broadcast_to(block[None], (size,) + block.shape)
    return lax.all_to_all(copies, axis, 0, 0)


def sum_rows(terms, axis, size):
    rows, cols = terms.shape
    pieces = lax.all_to_all(terms.reshape(size, rows // size, cols), axis, 0, 0)
    return jnp.sum(pieces.astype(F32), axis=0)


def swap_cores(block):
    return lax.ppermute(block, "core", [(0, 1), (1, 0)])


def gather_both_ways(block, n_y, n_x, is_first):
    def place(y, x, core):
        return (y * n_x + x) * 2 + core

    def along_x(core):
        return [[place(y, x, core) for x in range(n_x)] for y in range(n_y)]

    def along_y(core):
        return [[place(y, x, core) for y in range(n_y)] for x in range(n_x)]

    for groups in (along_x(0) + along_y(1), along_y(0) + along_x(1)):
        copies = jnp.broadcast_to(block[None], (len(groups[0]),) + block.shape)
        block = lax.all_to_all(copies, ("y", "x", "core"), 0, 0, axis_index_groups=groups)
    block = jnp.where(is_first, block, jnp.swapaxes(block, 0, 1))
    return block.reshape(-1, block.shape[-1])


def matmul(a, b, contract):
    return lax.dot_general(a, b, ((contract[0:1], contract[1:2]), ((), ())), preferred_element_type=F32)


def add_terms(terms_ref, out_ref, total_ref):
    @pl.when(pl.program_id(0) == 0)
    def _():
        total_ref[...] = jnp.zeros_like(total_ref)

    total = total_ref[...]
    for i in range(terms_ref.shape[0]):
        total += terms_ref[i].astype(F32)
    total_ref[...] = total

    @pl.when(pl.program_id(0) == pl.num_programs(0) - 1)
    def _():
        out_ref[...] = total_ref[...].astype(BF16)


def sum_terms(terms, at_once):
    count, rows, cols = terms.shape
    return pl.pallas_call(
        add_terms,
        grid=(count // at_once,),
        in_specs=[pl.BlockSpec((at_once, rows, cols), lambda i: (i, 0, 0))],
        out_specs=pl.BlockSpec((rows, cols), lambda i: (0, 0)),
        out_shape=jax.ShapeDtypeStruct((rows, cols), BF16),
        scratch_shapes=[pltpu.VMEM((rows, cols), F32)],
        compiler_params=pltpu.CompilerParams(vmem_limit_bytes=32 * 2**20),
        cost_estimate=pl.CostEstimate(
            flops=count * rows * cols, bytes_accessed=2 * (count + 1) * rows * cols, transcendentals=0
        ),
    )(terms)


def make_per_device(n_row, n_y, n_x, n_z, n_near):
    def per_device(factor_panel, solved_earlier, right_side, coupling, inverses):
        core = lax.axis_index("core")
        near = lax.axis_index("near")
        _, rows, _ = factor_panel.shape
        own = coupling.shape[1]
        part = rows // n_near
        is_first = core == 0

        depth = solved_earlier.shape[1]
        split = depth * SPLIT // 24
        earlier = lax.all_gather(solved_earlier[:, :split], ROW, axis=0, tiled=True)

        right = jnp.where(is_first, right_side[0], right_side[1])
        right = lax.dynamic_slice_in_dim(right, near * part, part, axis=0)
        packed = jnp.concatenate([coupling.T, inverses[0]], axis=0)
        rest = gather_both_ways(solved_earlier[:, split:], n_y, n_x, core == 0)
        packed, right, is_first, rest = lax.optimization_barrier((packed, right, is_first, rest))

        mine = spread(spread(packed, "far", n_z // n_near), "near", n_near).reshape(n_z, *packed.shape)
        other = swap_cores(mine)
        left = [
            matmul(inverses[1], part_[:, :own].reshape(-1, rows), (1, 1)).astype(BF16)
            for part_ in (mine, other)
        ]
        even = lax.axis_index("x") % 2 == 0
        pairs = [(x, x ^ 1) for x in range(n_x)]
        received = lax.ppermute(jnp.where(even, left[1], left[0]), "x", pairs)
        left = (jnp.where(even, left[0], left[1]).astype(F32) + received.astype(F32)).astype(BF16)
        quarters = lax.all_gather(left, ROW, axis=0, tiled=False)
        panel = factor_panel.reshape(2 * rows, depth)
        rest = matmul(panel[:, split:], rest, (1, 1))
        earlier, _, rest = lax.optimization_barrier((earlier, left, rest))

        terms = (rest + matmul(panel[:, :split], earlier, (1, 1))).reshape(2, rows, -1)
        kept = jnp.where(is_first, terms[0], terms[1])
        sent = jnp.where(is_first, terms[1], terms[0]).astype(BF16)
        kept = (kept + swap_cores(sent).astype(F32)).astype(BF16)
        quarter = sum_rows(kept, "near", n_near).astype(BF16)
        prefix = jnp.sum(spread(quarter, "far", n_z // n_near).astype(F32), axis=0)
        residual = (right.astype(F32) - prefix).astype(BF16)
        residual = spread(residual, "near", n_near).reshape(rows, -1)
        residual_other = swap_cores(residual)

        _, quarters = lax.optimization_barrier((residual, quarters))
        left = sum_terms(quarters.reshape(n_row // 2, 2 * own, -1), 4).reshape(2, own, -1)
        cross = -(
            matmul(left[0], mine[:, own:].reshape(-1, rows), (1, 0))
            + matmul(left[1], other[:, own:].reshape(-1, rows), (1, 0))
        )
        from_first = jnp.concatenate([inverses[0], cross.astype(BF16)], axis=0)
        from_second = jnp.concatenate([jnp.zeros_like(inverses[1]), inverses[1]], axis=0)
        weights_mine = jnp.where(is_first, from_first, from_second)
        weights_other = jnp.where(is_first, from_second, from_first)
        out = matmul(weights_mine, residual, (1, 0)) + matmul(weights_other, residual_other, (1, 0))
        out = sum_rows(out.astype(BF16), ROW, n_row).astype(BF16)
        return spread(out, ROW, n_row).reshape(2, own, -1)

    return per_device


def solution(mesh):
    n_row, n_col = mesh.shape["row"], mesh.shape["col"]
    n_x = 4
    n_y = n_row // n_x
    n_z = n_col // 2
    n_near = 4
    split = Mesh(mesh.devices.reshape(n_y, n_x, n_z // n_near, n_near, 2), ("y", "x", "far", "near", "core"))
    col = ("far", "near", "core")
    return jax.shard_map(
        make_per_device(n_row, n_y, n_x, n_z, n_near),
        mesh=split,
        in_specs=(
            P(None, ROW, col),
            P(ROW, col),
            P(None, ROW, None),
            P(ROW, col),
            P(None, col, ROW),
        ),
        out_specs=P(None, col, None),
        check_vma=False,
    )
```
